32 devices in a mesh: gx: 2 (over core), gy: 4 (over y, x), gz: 4 (over z).
Axes of the slice: x: 2, y: 2, z: 4, core: 2. Of those that a mesh axis runs over, the one named last changes fastest.
Arguments:
- resid_x: float32 [6, 8, 4, 120, 512], P('gx', 'gy', 'gz'), may hold values from -6 to 6
- resid_y: float32 [4, 12, 4, 120, 512], P('gx', 'gy', 'gz'), may hold values from -6 to 6
- face_weights: float32 [4, 8, 4, 4, 120], P('gx', 'gy', 'gz'), may hold values from 0.25 to 0.75
- face_counts: int32 [4, 8, 4, 4], P('gx', 'gy', 'gz'), may hold values from 1 to 4, as said below
- neumann: bfloat16 [4, 8, 4, 480, 480], P('gx', 'gy', 'gz'), may hold values from -0.25 to 0.25
- schur: bfloat16 [4, 8, 4, 480, 480], P('gx', 'gy', 'gz'), may hold values from -0.25 to 0.25
- basis: bfloat16 [4, 8, 4, 480, 64], P('gx', 'gy', 'gz'), may hold values from -0.25 to 0.25
- coarse_map: int32 [4, 8, 4, 64], P('gx', 'gy', 'gz'), may hold values from 0 to 511
- column_inverse: float32 [2, 4, 512, 512], P('gx', 'gy', 'gz'), may hold values from -0.25 to 0.25
- column_basis: float32 [2, 4, 512, 512], P('gx', 'gy', 'gz'), may hold values from -0.25 to 0.25
- top_inverse: float32 [512, 512], replicated, may hold values from -0.09375 to 0.09375
Outputs:
- z_x: float32 [6, 8, 4, 120, 512], P('gx', 'gy', 'gz')
- z_y: float32 [4, 12, 4, 120, 512], P('gx', 'gy', 'gz')
- schur_image: bfloat16 [4, 8, 4, 480, 512], P('gx', 'gy', 'gz')
The draws below stay inside these ranges and needn't reach their ends.
Inputs may be any that keep to these rules, and one draw needn't show every extreme that they name: `face_counts`: only the first 30 * count of a face's 120 dofs are live; about one face in eight has 4 live mesh faces. `coarse_map`: several local coarse dofs may share a column coarse dof.
All inputs are finite; a program needn't handle non-finite values.
Results may differ from the reference program's by a relative error of at most 0.0063.
Values sent between devices are 32-bit elements; how exact they have to be, the bound alone decides.
A program may use at most 64 MiB of HBM per device.

```python
import jax
import jax.numpy as jnp
from jax import lax

BLK = 30
MAXB = 4
FW = 120
NI = 480
LOAD_CASES = 512
COARSE_DOFS = 64
NC2 = 512
NC3 = 512
N_GX = 2
N_GY = 4
N_GZ = 4


def draw_face_counts(key, part):
    picks = jax.random.randint(key, (2 * N_GX, 2 * N_GY, N_GZ, 4), 0, 8)
    values = jnp.where(picks == 0, MAXB, jnp.where(picks == 1, 2, 1))
    flat = values.reshape(-1).at[0].set(MAXB).at[1].set(1)
    return flat.reshape(2 * N_GX, 2 * N_GY, N_GZ, 4).astype(jnp.int32)


def place_ends(drawn, rng, least, high):
    shape = drawn.shape
    index_at = [jax.random.randint(jax.random.fold_in(rng, axis), (), 0, shape[axis]) for axis in range(len(shape))]
    drawn = drawn.at[tuple(index_at)].set(least)
    longest = shape.index(max(shape))
    index_at[longest] = (index_at[longest] + 1) % shape[longest]
    return drawn.at[tuple(index_at)].set(high)


def block_scale(own_key, shape, pieces, least, largest):
    def one(dim, shards_of):
        steps = jax.random.uniform(jax.random.fold_in(jax.random.fold_in(own_key, 6), dim), (shards_of,), jnp.float32, least / len(pieces), largest / len(pieces))
        return jnp.repeat(jnp.exp(steps), shape[dim] // shards_of).reshape((-1,) + (1,) * (len(shape) - dim - 1))

    level = one(*pieces[0])
    for cut in pieces[1:]:
        level = level * one(*cut)
    return level


def normal_values(stream_key, extent, width, limit, shards=(), kind=jnp.bfloat16):
    values = jax.random.normal(stream_key, extent, jnp.float32) * width
    if len(shards) > 0:
        values = block_scale(stream_key, extent, shards, -0.22, 0.18) * values
    return jnp.clip(values, min=-limit, max=limit).astype(kind)


def setup_inputs(seed: int = 0) -> dict:
    arg_keys = jax.random.split(jax.random.key(seed), 12)
    resid_x = normal_values(arg_keys[0], (3 * N_GX, 2 * N_GY, N_GZ, FW, LOAD_CASES), 1.0, 6.0, ((0, 2), (1, 4), (2, 4)), jnp.float32)
    resid_y = normal_values(arg_keys[1], (2 * N_GX, 3 * N_GY, N_GZ, FW, LOAD_CASES), 1.0, 6.0, ((0, 2), (1, 4), (2, 4)), jnp.float32)
    face_weights = jnp.clip(0.25 + 0.5 * jax.random.uniform(arg_keys[2], (2 * N_GX, 2 * N_GY, N_GZ, 4, FW), jnp.float32) ** block_scale(arg_keys[2], (2 * N_GX, 2 * N_GY, N_GZ, 4, FW), ((0, 2), (1, 4), (2, 4)), -0.2, 0.2), 0.25, 0.75)
    face_counts = draw_face_counts(jax.random.fold_in(arg_keys[11], 71), 0)
    neumann = normal_values(arg_keys[4], (2 * N_GX, 2 * N_GY, N_GZ, NI, NI), NI ** -0.5, 0.25, ((0, 2), (1, 4), (2, 4)))
    schur = normal_values(arg_keys[5], (2 * N_GX, 2 * N_GY, N_GZ, NI, NI), NI ** -0.5, 0.25, ((0, 2), (1, 4), (2, 4)))
    basis = normal_values(arg_keys[6], (2 * N_GX, 2 * N_GY, N_GZ, NI, COARSE_DOFS), NI ** -0.5, 0.25, ((0, 2), (1, 4), (2, 4)))
    coarse_map = place_ends(jax.random.randint(arg_keys[7], (2 * N_GX, 2 * N_GY, N_GZ, COARSE_DOFS), 0, NC2), jax.random.fold_in(arg_keys[7], 1), 0, NC2 - 1).astype(jnp.int32)
    column_inverse = normal_values(arg_keys[8], (N_GX, N_GY, NC2, NC2), NC2 ** -0.5, 0.25, ((0, 2), (1, 4), (2, 4)), jnp.float32)
    column_basis = normal_values(arg_keys[9], (N_GX, N_GY, NC2, NC3), NC2 ** -0.5, 0.25, ((0, 2), (1, 4), (2, 4)), jnp.float32)
    top_inverse = normal_values(arg_keys[10], (NC3, NC3), (NC3 * N_GX * N_GY) ** -0.5, 0.09375, (), jnp.float32)
    return {"resid_x": resid_x, "resid_y": resid_y, "face_weights": face_weights, "face_counts": face_counts, "neumann": neumann, "schur": schur, "basis": basis, "coarse_map": coarse_map, "column_inverse": column_inverse, "column_basis": column_basis, "top_inverse": top_inverse}


def physical_x(copies):
    rows = copies.reshape(N_GX, 3, 2 * N_GY, N_GZ, FW, LOAD_CASES)
    even = rows[:, 0] + jnp.roll(rows[:, 2], 1, axis=0)
    return jnp.stack([even, rows[:, 1]], 1).reshape(2 * N_GX, 2 * N_GY, N_GZ, FW, LOAD_CASES)


def physical_y(copies):
    rows = copies.reshape(2 * N_GX, N_GY, 3, N_GZ, FW, LOAD_CASES)
    even = rows[:, :, 0] + jnp.roll(rows[:, :, 2], 1, axis=1)
    return jnp.stack([even, rows[:, :, 1]], 2).reshape(2 * N_GX, 2 * N_GY, N_GZ, FW, LOAD_CASES)


def copies_x(faces):
    rows = faces.reshape(N_GX, 2, 2 * N_GY, N_GZ, FW, LOAD_CASES)
    stacked = jnp.stack([rows[:, 0], rows[:, 1], jnp.roll(rows[:, 0], -1, axis=0)], 1)
    return stacked.reshape(3 * N_GX, 2 * N_GY, N_GZ, FW, LOAD_CASES)


def copies_y(faces):
    rows = faces.reshape(2 * N_GX, N_GY, 2, N_GZ, FW, LOAD_CASES)
    stacked = jnp.stack([rows[:, :, 0], rows[:, :, 1], jnp.roll(rows[:, :, 0], -1, axis=1)], 2)
    return stacked.reshape(2 * N_GX, 3 * N_GY, N_GZ, FW, LOAD_CASES)


def sub_faces(face_x, face_y):
    return jnp.stack([face_x, jnp.roll(face_x, -1, axis=0), face_y, jnp.roll(face_y, -1, axis=1)], 3)


def to_columns(array):
    tail = array.shape[3:]
    moved = array.reshape((N_GX, 2, N_GY, 2, N_GZ) + tail).transpose((0, 2, 1, 3, 4) + tuple(range(5, 5 + len(tail))))
    return moved.reshape((N_GX, N_GY, 4 * N_GZ * tail[0]) + tail[1:])


def reference(resid_x, resid_y, face_weights, face_counts, neumann, schur, basis, coarse_map, column_inverse, column_basis, top_inverse):
    subdomain_count = 4 * N_GX * N_GY * N_GZ
    high = lax.Precision.HIGHEST
    dof_index = jnp.arange(FW, dtype=jnp.int32)
    live = (dof_index[None, None, None, None, :] < face_counts[..., None] * BLK).astype(jnp.float32)
    scale = face_weights * live
    faces = sub_faces(physical_x(resid_x), physical_y(resid_y))
    upart = (faces * scale[..., None]).reshape(subdomain_count, NI, LOAD_CASES).astype(jnp.bfloat16)
    nflat = neumann.reshape(subdomain_count, NI, NI)
    basis_flattened = basis.reshape(subdomain_count, NI, COARSE_DOFS)

    def first(items):
        vec, nmat, bmat = items
        wvec = jnp.dot(nmat, vec, preferred_element_type=jnp.float32)
        gvec = jnp.dot(bmat.T, vec, preferred_element_type=jnp.float32)
        return wvec, gvec

    weight_total, gall = lax.map(first, (upart, nflat, basis_flattened))
    gcol = to_columns(gall.reshape(2 * N_GX, 2 * N_GY, N_GZ, COARSE_DOFS, LOAD_CASES))
    mcol = to_columns(coarse_map.reshape(2 * N_GX, 2 * N_GY, N_GZ, COARSE_DOFS, 1))[..., 0]

    def scatter_one(target, values):
        return jnp.zeros((NC2, LOAD_CASES), jnp.float32).at[target].add(values)

    g2 = jax.vmap(jax.vmap(scatter_one))(mcol, gcol)
    y2 = jnp.einsum('abrk,abkn->abrn', column_inverse, g2, precision=high)
    g3 = jnp.einsum('abrk,abrn->kn', column_basis, g2, precision=high)
    y3 = jnp.dot(top_inverse, g3, precision=high)
    v2 = y2 + jnp.einsum('abrk,kn->abrn', column_basis, y3, precision=high)
    value_column = jnp.take_along_axis(v2, mcol[..., None], axis=2)
    subdomain_values = value_column.reshape(N_GX, N_GY, 2, 2, N_GZ, COARSE_DOFS, LOAD_CASES).transpose(0, 2, 1, 3, 4, 5, 6)
    subdomain_values = subdomain_values.reshape(subdomain_count, COARSE_DOFS, LOAD_CASES).astype(jnp.bfloat16)

    def second_level(items):
        wvec, bmat, coarse = items
        return wvec + jnp.dot(bmat, coarse, preferred_element_type=jnp.float32)

    output_total = lax.map(second_level, (weight_total, basis_flattened, subdomain_values))
    contrib = output_total.reshape(2 * N_GX, 2 * N_GY, N_GZ, 4, FW, LOAD_CASES) * scale[..., None]
    zphys_x = contrib[:, :, :, 0] + jnp.roll(contrib[:, :, :, 1], 1, axis=0)
    zphys_y = contrib[:, :, :, 2] + jnp.roll(contrib[:, :, :, 3], 1, axis=1)
    z_x = copies_x(zphys_x)
    z_y = copies_y(zphys_y)
    zsub = (sub_faces(zphys_x, zphys_y) * live[..., None]).reshape(subdomain_count, NI, LOAD_CASES).astype(jnp.bfloat16)

    def third(items):
        vec, smat = items
        return jnp.dot(smat, vec, preferred_element_type=jnp.float32).astype(jnp.bfloat16)

    image = lax.map(third, (zsub, schur.reshape(subdomain_count, NI, NI)))
    return z_x, z_y, image.reshape(2 * N_GX, 2 * N_GY, N_GZ, NI, LOAD_CASES)
```

```python
import functools

import jax
import jax.numpy as jnp
from jax import lax
from jax.experimental import pallas as pl
from jax.experimental.pallas import tpu as pltpu
from jax.sharding import PartitionSpec as P

BLK = 30
AXES = ("gx", "gy", "gz")
MESH = pl.DeviceIdType.MESH
F32 = jnp.float32
BF16 = jnp.bfloat16


def mm(a, b):
    return jnp.dot(a.astype(BF16), b.astype(BF16), preferred_element_type=F32)


def mm_t(a, b):
    return lax.dot_general(
        a.astype(BF16), b.astype(BF16), (((0,), (0,)), ((), ())), preferred_element_type=F32
    )


def kernel(
    sizes,
    owners,
    rx,
    ry,
    scale,
    live,
    neumann,
    schur,
    basis,
    cmap,
    inv,
    cbas,
    top,
    zx,
    zy,
    image,
    hx1,
    hy1,
    hx2,
    hy2,
    ubuf,
    wbuf,
    graw,
    raw,
    maps,
    minv,
    mbas,
    g3p,
    rs,
    part,
    g3,
    vout,
    vall,
    h1_s,
    h1_r,
    h2_s,
    h2_r,
    mat_s,
    mat_r,
    raw_s,
    raw_r,
    rs_s,
    rs_r,
    ag_s,
    ag_r,
    v_s,
    v_r,
):
    gx_n, gy_n, gz_n = sizes
    x, y, z = (lax.axis_index(a) for a in AXES)
    layer_n = gx_n * gy_n
    mine = x * gy_n + y
    halves = len(owners)
    width = rx.shape[3] // halves
    ni, nj = rx.shape[0] - 1, ry.shape[1] - 1
    coarse = basis.shape[2]
    rows = inv.shape[0]
    slab = part.shape[0]

    def cols(h):
        return slice(h * width, (h + 1) * width)

    def copy(src, dst, send, recv, to):
        return pltpu.make_async_remote_copy(
            src_ref=src, dst_ref=dst, send_sem=send, recv_sem=recv, device_id=to, device_id_type=MESH
        )

    def layer_peer(d):
        p = lax.rem(mine + d, layer_n)
        return (p // gy_n, lax.rem(p, gy_n), z)

    barrier = pltpu.get_barrier_semaphore()
    for d in range(1, layer_n):
        pl.semaphore_signal(barrier, inc=1, device_id=layer_peer(d), device_id_type=MESH)
    for d in range(1, gz_n):
        pl.semaphore_signal(
            barrier, inc=1, device_id=(x, y, lax.rem(z + d, gz_n)), device_id_type=MESH
        )
    pl.semaphore_wait(barrier, layer_n - 1 + gz_n - 1)

    x_up, x_down = (lax.rem(x + 1, gx_n), y, z), (lax.rem(x + gx_n - 1, gx_n), y, z)
    y_up, y_down = (x, lax.rem(y + 1, gy_n), z), (x, lax.rem(y + gy_n - 1, gy_n), z)

    def halo(fx, fy, hx, hy, send, recv, h):
        c = cols(h)
        s, r = send.at[h], recv.at[h]
        return [
            copy(fy.at[:, nj, :, c], hy.at[0, :, :, c], s.at[0], r.at[0], y_up),
            copy(fy.at[:, 0, :, c], hy.at[1, :, :, c], s.at[1], r.at[1], y_down),
            copy(fx.at[ni, :, :, c], hx.at[0, :, :, c], s.at[2], r.at[2], x_up),
            copy(fx.at[0, :, :, c], hx.at[1, :, :, c], s.at[3], r.at[3], x_down),
        ]

    own_rows = pl.ds(pl.multiple_of(z * rows, rows), rows)

    def matrices(k):
        to = (x, y, owners[k])
        return [
            copy(inv, minv.at[own_rows], mat_s.at[k, 0], mat_r.at[0, z], to),
            copy(cbas, mbas.at[own_rows], mat_s.at[k, 1], mat_r.at[1, z], to),
            copy(cmap, maps.at[z], mat_s.at[k, 2], mat_r.at[2, z], to),
        ]

    first = [halo(rx, ry, hx1, hy1, h1_s, h1_r, h) for h in range(halves)]
    for c in first[0]:
        c.start()
    for k in range(halves):

        @pl.when(z != owners[k])
        def _():
            for c in matrices(k):
                c.start()

        @pl.when(z == owners[k])
        def _():
            minv[own_rows] = inv[...]
            mbas[own_rows] = cbas[...]
            maps[z] = cmap[...]

    for h in range(1, halves):
        for c in first[h]:
            c.start()

    def stack_faces(xf, yf, i, j):
        return jnp.concatenate([xf(i, j), xf(i + 1, j), yf(i, j), yf(i, j + 1)], 0)

    for h in range(halves):
        c = cols(h)
        for f in first[h]:
            f.wait_recv()

        def xf(q, j):
            own = rx[q, j, :, c]
            return own if 0 < q < ni else own + hx1[0 if q == 0 else 1, j, :, c]

        def yf(i, q):
            own = ry[i, q, :, c]
            return own if 0 < q < nj else own + hy1[0 if q == 0 else 1, i, :, c]

        for i in range(ni):
            for j in range(nj):
                s = i * nj + j
                u = (stack_faces(xf, yf, i, j) * scale[s]).astype(BF16)
                ubuf[s, :, c] = u
                graw[h, s * coarse : (s + 1) * coarse] = mm_t(basis[s], u)
        o = owners[h]

        @pl.when(z != o)
        def _():
            copy(graw.at[h], raw.at[z], raw_s.at[h], raw_r.at[z], (x, y, o)).start()

        @pl.when(z == o)
        def _():
            raw[z] = graw[h]

    for s in range(ni * nj):
        wbuf[s] = jnp.dot(neumann[s], ubuf[s], preferred_element_type=F32)

    def select(zz):
        picks = lax.broadcasted_iota(jnp.int32, (minv.shape[0], cmap.shape[1]), 0)
        return (picks == maps[zz, 0:1]).astype(F32).astype(BF16)

    which = z - owners[0]

    def back(zz):
        return copy(vout.at[zz], vall.at[which], v_s.at[zz], v_r.at[which], (x, y, zz))

    @pl.when((z >= owners[0]) & (z <= owners[-1]))
    def _():
        for zz in range(gz_n):

            @pl.when(z != zz)
            def _():
                copy(graw.at[0], raw.at[zz], raw_s.at[0], raw_r.at[zz], (x, y, zz)).wait_recv()
                there = pl.ds(zz * rows, rows)
                copy(cmap, maps.at[zz], mat_s.at[0, 2], mat_r.at[2, zz], (x, y, zz)).wait_recv()
                copy(inv, minv.at[there], mat_s.at[0, 0], mat_r.at[0, zz], (x, y, zz)).wait_recv()
                copy(cbas, mbas.at[there], mat_s.at[0, 1], mat_r.at[1, zz], (x, y, zz)).wait_recv()

        g2 = lax.fori_loop(
            0,
            gz_n,
            lambda zz, acc: acc + mm(select(zz), raw[zz]),
            jnp.zeros((minv.shape[0], width), F32),
        ).astype(BF16)
        g3p[...] = mm_t(mbas[...], g2)

        def scatter(d):
            to = layer_peer(d)
            there = pl.ds(pl.multiple_of((to[0] * gy_n + to[1]) * slab, slab), slab)
            return copy(g3p.at[there], rs.at[d - 1], rs_s.at[d - 1], rs_r.at[d - 1], to)

        own_slab = pl.ds(pl.multiple_of(mine * slab, slab), slab)

        def gather(d):
            return copy(part, g3.at[own_slab], ag_s.at[d - 1], ag_r.at[d - 1], layer_peer(d))

        def gathered(d):
            q = lax.rem(mine + layer_n - d, layer_n)
            there = pl.ds(pl.multiple_of(q * slab, slab), slab)
            return copy(part, g3.at[there], ag_s.at[d - 1], ag_r.at[d - 1], layer_peer(d))

        for d in range(1, layer_n):
            scatter(d).start()
        y2 = mm(minv[...], g2)
        total = g3p[own_slab]
        for d in range(1, layer_n):
            scatter(d).wait_recv()
            total = total + rs[d - 1]
        part[...] = total
        g3[own_slab] = total
        for d in range(1, layer_n):
            gather(d).start()
        for d in range(1, layer_n):
            gathered(d).wait_recv()
        y3 = mm(top[...], g3[...])
        v2 = (y2 + mm(mbas[...], y3)).astype(BF16)
        for zz in range(gz_n):
            vout[zz] = mm_t(select(zz), v2)

            @pl.when(z != zz)
            def _():
                back(zz).start()

            @pl.when(z == zz)
            def _():
                vall[which] = vout[zz]

        for d in range(1, layer_n):
            scatter(d).wait_send()
            gather(d).wait_send()

    second = [halo(zx, zy, hx2, hy2, h2_s, h2_r, h) for h in range(halves)]
    for h in range(halves):
        c = cols(h)
        o = owners[h]

        @pl.when(z != o)
        def _():
            copy(vout.at[0], vall.at[h], v_s.at[0], v_r.at[h], (x, y, o)).wait_recv()

        face = rx.shape[2]
        for i in range(ni):
            for j in range(nj):
                s = i * nj + j
                v = vall[h, s * coarse : (s + 1) * coarse].astype(BF16)
                con = (
                    wbuf[s, :, c] + jnp.dot(basis[s], v, preferred_element_type=F32)
                ) * scale[s]
                c0, c1, c2, c3 = (con[k * face : (k + 1) * face] for k in range(4))
                zx[i, j, :, c] = c0 if i == 0 else zx[i, j, :, c] + c0
                zx[i + 1, j, :, c] = c1
                zy[i, j, :, c] = c2 if j == 0 else zy[i, j, :, c] + c2
                zy[i, j + 1, :, c] = c3
        for f in second[h]:
            f.start()

    for h in range(halves):
        c = cols(h)
        for f in second[h]:
            f.wait()
        for j in range(nj):
            zx[0, j, :, c] += hx2[0, j, :, c]
            zx[ni, j, :, c] += hx2[1, j, :, c]
        for i in range(ni):
            zy[i, 0, :, c] += hy2[0, i, :, c]
            zy[i, nj, :, c] += hy2[1, i, :, c]
        for i in range(ni):
            for j in range(nj):
                s = i * nj + j
                zs = stack_faces(
                    lambda q, jj: zx[q, jj, :, c], lambda ii, q: zy[ii, q, :, c], i, j
                )
                zs = (zs * live[s]).astype(BF16)
                image[s, :, c] = jnp.dot(schur[s], zs, preferred_element_type=F32).astype(BF16)

    for h in range(halves):
        for f in first[h]:
            f.wait_send()
        o = owners[h]

        @pl.when(z != o)
        def _():
            for f in matrices(h):
                f.wait_send()
            copy(graw.at[h], raw.at[z], raw_s.at[h], raw_r.at[z], (x, y, o)).wait_send()

    @pl.when((z >= owners[0]) & (z <= owners[-1]))
    def _():
        for zz in range(gz_n):

            @pl.when(z != zz)
            def _():
                back(zz).wait_send()


def on_device(
    sizes,
    resid_x,
    resid_y,
    face_weights,
    face_counts,
    neumann,
    schur,
    basis,
    coarse_map,
    column_inverse,
    column_basis,
    top_inverse,
):
    gx_n, gy_n, gz_n = sizes
    layer_n = gx_n * gy_n
    owners = ((gz_n - 1) // 2, gz_n // 2) if gz_n % 2 == 0 else (gz_n // 2,)
    halves = len(owners)
    face, loads = resid_x.shape[3:]
    inner = neumann.shape[3]
    coarse = basis.shape[4]
    subs = neumann.shape[0] * neumann.shape[1]
    rx = resid_x[:, :, 0]
    ry = resid_y[:, :, 0]
    dof = jnp.arange(face, dtype=jnp.int32)
    live = (dof < face_counts[:, :, 0, :, None] * BLK).astype(F32)
    scale = (face_weights[:, :, 0] * live).reshape(subs, inner, 1)
    live = live.reshape(subs, inner, 1)
    local = subs * coarse
    cmap = jnp.broadcast_to(coarse_map.reshape(1, local), (8, local))
    inv, cbas = column_inverse[0, 0], column_basis[0, 0]
    nc2, nc3 = inv.shape[1], top_inverse.shape[0]
    width = loads // halves
    slab = nc3 // layer_n
    dma = pltpu.SemaphoreType.DMA
    vm = pltpu.VMEM
    nx, ny = rx.shape[1], ry.shape[0]
    spec = pl.BlockSpec(memory_space=pltpu.VMEM)
    z_x, z_y, image = pl.pallas_call(
        functools.partial(kernel, sizes, owners),
        out_shape=(
            jax.ShapeDtypeStruct(rx.shape, F32),
            jax.ShapeDtypeStruct(ry.shape, F32),
            jax.ShapeDtypeStruct((subs, inner, loads), BF16),
        ),
        in_specs=[spec] * 11,
        out_specs=(spec,) * 3,
        scratch_shapes=[
            vm((2, nx, face, loads), F32),
            vm((2, ny, face, loads), F32),
            vm((2, nx, face, loads), F32),
            vm((2, ny, face, loads), F32),
            vm((subs, inner, loads), BF16),
            vm((subs, inner, loads), F32),
            vm((halves, local, width), F32),
            vm((gz_n, local, width), F32),
            vm((gz_n, 8, local), jnp.int32),
            vm((nc2, nc2), F32),
            vm((nc2, nc3), F32),
            vm((nc3, width), F32),
            vm((layer_n - 1, slab, width), F32),
            vm((slab, width), F32),
            vm((nc3, width), F32),
            vm((gz_n, local, width), F32),
            vm((halves, local, width), F32),
            dma((halves, 4)),
            dma((halves, 4)),
            dma((halves, 4)),
            dma((halves, 4)),
            dma((halves, 3)),
            dma((3, gz_n)),
            dma((halves,)),
            dma((gz_n,)),
            dma((layer_n - 1,)),
            dma((layer_n - 1,)),
            dma((layer_n - 1,)),
            dma((layer_n - 1,)),
            dma((gz_n,)),
            dma((halves,)),
        ],
        compiler_params=pltpu.CompilerParams(
            collective_id=0, has_side_effects=True, vmem_limit_bytes=56 * 1024 * 1024
        ),
        name="bddc",
    )(
        rx,
        ry,
        scale,
        live,
        neumann.reshape(subs, inner, inner),
        schur.reshape(subs, inner, inner),
        basis.reshape(subs, inner, coarse),
        cmap,
        inv,
        cbas,
        top_inverse,
    )
    return (
        z_x[:, :, None],
        z_y[:, :, None],
        image.reshape(neumann.shape[0], neumann.shape[1], 1, inner, loads),
    )


def solution(mesh):
    sizes = tuple(mesh.shape[a] for a in AXES)
    vec, mat = P("gx", "gy", "gz", None), P("gx", "gy", "gz", None, None)
    return jax.shard_map(
        functools.partial(on_device, sizes),
        mesh=mesh,
        in_specs=(mat, mat, mat, vec, mat, mat, mat, vec, vec, vec, P()),
        out_specs=(mat, mat, mat),
        check_vma=False,
    )
```

```python
import functools

import jax
import jax.numpy as jnp
from jax import lax
from jax.experimental import pallas as pl
from jax.experimental.pallas import tpu as pltpu
from jax.sharding import PartitionSpec as P

BLK = 30
AXES = ("gx", "gy", "gz")
MESH = pl.DeviceIdType.MESH
F32 = jnp.float32
BF16 = jnp.bfloat16


def mm(a, b):
    return jnp.dot(a.astype(BF16), b.astype(BF16), preferred_element_type=F32)


def live_mask(counts, i, j, face):
    index = lax.broadcasted_iota(jnp.int32, (face, counts.shape[2]), 0)
    return (index < counts[i, j : j + 1] * BLK).astype(F32)


def column(faces):
    return jnp.concatenate([faces[:, k : k + 1] for k in range(faces.shape[1])], 0)


def stack_faces(xf, yf, i, j):
    return jnp.concatenate([xf(i, j), xf(i + 1, j), yf(i, j), yf(i, j + 1)], 0)


def mm_t(a, b):
    return lax.dot_general(
        a.astype(BF16), b.astype(BF16), (((0,), (0,)), ((), ())), preferred_element_type=F32
    )


def kernel(
    sizes,
    owners,
    rx_hbm,
    ry_hbm,
    weights,
    counts,
    neumann_hbm,
    basis,
    targets,
    inv,
    cbas,
    top_hbm,
    zx,
    zy,
    rx,
    ry,
    neumann,
    top,
    scale,
    cmap,
    hx1,
    hy1,
    hx2,
    hy2,
    ubuf,
    wbuf,
    graw,
    raw,
    maps,
    minv,
    mbas,
    g3p,
    rs1,
    sum1,
    rs2,
    part,
    g3,
    vout,
    vall,
    h1_s,
    h1_r,
    h2_s,
    h2_r,
    mat_s,
    mat_r,
    raw_s,
    raw_r,
    rs1_s,
    rs1_r,
    rs2_s,
    rs2_r,
    ag1_s,
    ag1_r,
    ag2_s,
    ag2_r,
    v_s,
    v_r,
    in_s,
):
    gx_n, gy_n, gz_n = sizes
    x, y, z = (lax.axis_index(a) for a in AXES)
    layer_n = gx_n * gy_n
    mine = x * gy_n + y
    halves = len(owners)
    width = rx.shape[3] // halves
    ni, nj = rx.shape[0] - 1, ry.shape[1] - 1
    coarse = basis.shape[2]
    rows = inv.shape[0]
    slab = part.shape[0]

    def cols(h):
        return pl.ds(pl.multiple_of(h * width, width), width)

    def copy(src, dst, send, recv, to):
        return pltpu.make_async_remote_copy(
            src_ref=src, dst_ref=dst, send_sem=send, recv_sem=recv, device_id=to, device_id_type=MESH
        )

    def layer_peer(d):
        p = lax.rem(mine + d, layer_n)
        return (p // gy_n, lax.rem(p, gy_n), z)

    loads_in = [
        pltpu.make_async_copy(a, b, in_s.at[k])
        for k, (a, b) in enumerate(
            ((rx_hbm, rx), (ry_hbm, ry), (neumann_hbm, neumann), (top_hbm, top))
        )
    ]
    for c in loads_in:
        c.start()
    lists = [targets[i, j : j + 1] for i in range(ni) for j in range(nj)]
    cmap[...] = jnp.broadcast_to(jnp.concatenate(lists, 1), cmap.shape)

    barrier = pltpu.get_barrier_semaphore()
    for d in range(1, layer_n):
        pl.semaphore_signal(barrier, inc=1, device_id=layer_peer(d), device_id_type=MESH)
    for d in range(1, gz_n):
        pl.semaphore_signal(
            barrier, inc=1, device_id=(x, y, lax.rem(z + d, gz_n)), device_id_type=MESH
        )
    pl.semaphore_wait(barrier, layer_n - 1 + gz_n - 1)

    x_up, x_down = (lax.rem(x + 1, gx_n), y, z), (lax.rem(x + gx_n - 1, gx_n), y, z)
    y_up, y_down = (x, lax.rem(y + 1, gy_n), z), (x, lax.rem(y + gy_n - 1, gy_n), z)

    def halo(fx, fy, hx, hy, send, recv, h):
        c = cols(h)
        s, r = send.at[h], recv.at[h]
        return [
            copy(fy.at[:, nj, :, c], hy.at[0, :, :, c], s.at[0], r.at[0], y_up),
            copy(fy.at[:, 0, :, c], hy.at[1, :, :, c], s.at[1], r.at[1], y_down),
            copy(fx.at[ni, :, :, c], hx.at[0, :, :, c], s.at[2], r.at[2], x_up),
            copy(fx.at[0, :, :, c], hx.at[1, :, :, c], s.at[3], r.at[3], x_down),
        ]

    own_rows = pl.ds(pl.multiple_of(z * rows, rows), rows)

    def matrices(k):
        to = (x, y, owners[k])
        return [
            copy(inv, minv.at[own_rows], mat_s.at[k, 0], mat_r.at[0, z], to),
            copy(cbas, mbas.at[own_rows], mat_s.at[k, 1], mat_r.at[1, z], to),
            copy(cmap, maps.at[z], mat_s.at[k, 2], mat_r.at[2, z], to),
        ]

    first = [halo(rx_hbm, ry_hbm, hx1, hy1, h1_s, h1_r, h) for h in range(halves)]
    for c in first[0]:
        c.start()
    for k in range(halves):

        @pl.when(z != owners[k])
        def _():
            for c in matrices(k):
                c.start()

        @pl.when(z == owners[k])
        def _():
            minv[own_rows] = inv[...]
            mbas[own_rows] = cbas[...]
            maps[z] = cmap[...]

    for h in range(1, halves):
        for c in first[h]:
            c.start()

    for i in range(ni):
        for j in range(nj):
            scale[i * nj + j] = column(weights[i, j].T * live_mask(counts, i, j, rx.shape[2]))
    loads_in[0].wait()
    loads_in[1].wait()

    for h in range(halves):
        c = cols(h)
        for f in first[h]:
            f.wait_recv()

        def xf(q, j):
            own = rx[q, j, :, c]
            return own if 0 < q < ni else own + hx1[0 if q == 0 else 1, j, :, c]

        def yf(i, q):
            own = ry[i, q, :, c]
            return own if 0 < q < nj else own + hy1[0 if q == 0 else 1, i, :, c]

        for i in range(ni):
            for j in range(nj):
                s = i * nj + j
                u = (stack_faces(xf, yf, i, j) * scale[s]).astype(BF16)
                ubuf[s, :, c] = u
                graw[h, s * coarse : (s + 1) * coarse] = mm_t(basis[s], u)
        o = owners[h]

        @pl.when(z != o)
        def _():
            copy(graw.at[h], raw.at[z], raw_s.at[h], raw_r.at[z], (x, y, o)).start()

        @pl.when(z == o)
        def _():
            raw[z] = graw[h]

    loads_in[2].wait()
    for s in range(ni * nj):
        wbuf[s] = jnp.dot(neumann[s], ubuf[s], preferred_element_type=F32)

    def select(zz):
        picks = lax.broadcasted_iota(jnp.int32, (minv.shape[0], cmap.shape[1]), 0)
        return (picks == maps[zz, 0:1]).astype(F32).astype(BF16)

    loads_in[3].wait()
    which = z - owners[0]
    is_owner = (z >= owners[0]) & (z <= owners[-1])

    def far(zz):
        if zz < owners[0]:
            return z > owners[0]
        return z < owners[-1] if zz > owners[-1] else z < 0

    def back(zz):
        return copy(vout.at[zz], vall.at[which], v_s.at[zz], v_r.at[which], (x, y, zz))

    @pl.when(is_owner)
    def _():
        for zz in range(gz_n):

            @pl.when(z != zz)
            def _():
                copy(graw.at[0], raw.at[zz], raw_s.at[0], raw_r.at[zz], (x, y, zz)).wait_recv()
                there = pl.ds(zz * rows, rows)
                copy(cmap, maps.at[zz], mat_s.at[0, 2], mat_r.at[2, zz], (x, y, zz)).wait_recv()
                copy(inv, minv.at[there], mat_s.at[0, 0], mat_r.at[0, zz], (x, y, zz)).wait_recv()
                copy(cbas, mbas.at[there], mat_s.at[0, 1], mat_r.at[1, zz], (x, y, zz)).wait_recv()

        g2 = lax.fori_loop(
            0,
            gz_n,
            lambda zz, acc: acc + mm(select(zz), raw[zz]),
            jnp.zeros((minv.shape[0], width), F32),
        ).astype(BF16)
        g3p[...] = mm_t(mbas[...], g2)

        def x_peer(d):
            return (lax.rem(x + d, gx_n), y, z)

        def y_peer(d):
            return (x, lax.rem(y + d, gy_n), z)

        half = slab * gy_n
        own_half = pl.ds(pl.multiple_of(x * half, half), half)
        own_part = pl.ds(pl.multiple_of(y * slab, slab), slab)
        own_slab = pl.ds(pl.multiple_of(mine * slab, slab), slab)

        def scatter_x(d):
            to = x_peer(d)
            there = pl.ds(pl.multiple_of(to[0] * half, half), half)
            return copy(g3p.at[there], rs1.at[d - 1], rs1_s.at[d - 1], rs1_r.at[d - 1], to)

        def scatter_y(d):
            to = y_peer(d)
            there = pl.ds(pl.multiple_of(to[1] * slab, slab), slab)
            return copy(sum1.at[there], rs2.at[d - 1], rs2_s.at[d - 1], rs2_r.at[d - 1], to)

        def gather_y(d, source):
            rows_y = pl.ds(pl.multiple_of((x * gy_n + source) * slab, slab), slab)
            return copy(part, g3.at[rows_y], ag1_s.at[d - 1], ag1_r.at[d - 1], y_peer(d))

        def gather_x(d, source):
            rows_x = pl.ds(pl.multiple_of(source * half, half), half)
            return copy(g3.at[own_half], g3.at[rows_x], ag2_s.at[d - 1], ag2_r.at[d - 1], x_peer(d))

        for d in range(1, gx_n):
            scatter_x(d).start()
        y2 = mm(minv[...], g2)
        total = g3p[own_half]
        for d in range(1, gx_n):
            scatter_x(d).wait_recv()
            total = total + rs1[d - 1]
        sum1[...] = total
        for d in range(1, gy_n):
            scatter_y(d).start()
        total = sum1[own_part]
        for d in range(1, gy_n):
            scatter_y(d).wait_recv()
            total = total + rs2[d - 1]
        part[...] = total
        g3[own_slab] = total
        for d in range(1, gy_n):
            gather_y(d, y).start()
        for d in range(1, gy_n):
            gather_y(d, lax.rem(y + gy_n - d, gy_n)).wait_recv()
        for d in range(1, gx_n):
            gather_x(d, x).start()
        for d in range(1, gx_n):
            gather_x(d, lax.rem(x + gx_n - d, gx_n)).wait_recv()
        y3 = mm(top[...], g3[...])
        v2 = (y2 + mm(mbas[...], y3)).astype(BF16)
        for zz in range(gz_n):
            vout[zz] = mm_t(select(zz), v2)

            @pl.when((z != zz) & jnp.logical_not(far(zz)))
            def _():
                back(zz).start()

            @pl.when(z == zz)
            def _():
                vall[which] = vout[zz]

        for d in range(1, gx_n):
            scatter_x(d).wait_send()
            gather_x(d, x).wait_send()
        for d in range(1, gy_n):
            scatter_y(d).wait_send()
            gather_y(d, y).wait_send()

    turn = z // ((gz_n + 1) // 2) if halves > 1 else 0
    order = [lax.rem(k + turn, halves) for k in range(halves)]
    second = [halo(zx, zy, hx2, hy2, h2_s, h2_r, h) for h in order]
    face = rx.shape[2]
    for k, h in enumerate(order):
        c = cols(h)
        o = owners[0] + h

        @pl.when(z != o)
        def _():
            copy(vout.at[0], vall.at[h], v_s.at[0], v_r.at[h], (x, y, o)).wait_recv()

        for i in range(ni):
            for j in range(nj):
                s = i * nj + j
                v = vall[h, s * coarse : (s + 1) * coarse].astype(BF16)
                con = (
                    wbuf[s, :, c] + jnp.dot(basis[s], v, preferred_element_type=F32)
                ) * scale[s]
                c0, c1, c2, c3 = (con[k * face : (k + 1) * face] for k in range(4))
                zx[i, j, :, c] = c0 if i == 0 else zx[i, j, :, c] + c0
                zx[i + 1, j, :, c] = c1
                zy[i, j, :, c] = c2 if j == 0 else zy[i, j, :, c] + c2
                zy[i, j + 1, :, c] = c3
        for f in second[k]:
            f.start()
        if k == 0:

            @pl.when(is_owner)
            def _():
                for zz in range(gz_n):

                    @pl.when((z != zz) & jnp.logical_not(far(zz)))
                    def _():
                        back(zz).wait_send()

                for zz in range(gz_n):

                    @pl.when(far(zz))
                    def _():
                        back(zz).start()

    for k, h in enumerate(order):
        c = cols(h)
        for f in second[k]:
            f.wait()
        for j in range(nj):
            zx[0, j, :, c] += hx2[0, j, :, c]
            zx[ni, j, :, c] += hx2[1, j, :, c]
        for i in range(ni):
            zy[i, 0, :, c] += hy2[0, i, :, c]
            zy[i, nj, :, c] += hy2[1, i, :, c]

    for h in range(halves):
        for f in first[h]:
            f.wait_send()
        o = owners[h]

        @pl.when(z != o)
        def _():
            for f in matrices(h):
                f.wait_send()
            copy(graw.at[h], raw.at[z], raw_s.at[h], raw_r.at[z], (x, y, o)).wait_send()

    @pl.when(is_owner)
    def _():
        for zz in range(gz_n):

            @pl.when(far(zz))
            def _():
                back(zz).wait_send()


def image_kernel(zx, zy, counts, schur, out_x, out_y, image):
    out_x[...] = zx[...]
    out_y[...] = zy[...]
    ni, nj = zx.shape[0] - 1, zy.shape[1] - 1
    for i in range(ni):
        for j in range(nj):
            s = i * nj + j
            zs = stack_faces(lambda q, jj: zx[q, jj], lambda ii, q: zy[ii, q], i, j)
            zs = (zs * column(live_mask(counts, i, j, zx.shape[2]))).astype(BF16)
            image[s] = jnp.dot(schur[s], zs, preferred_element_type=F32).astype(BF16)


def on_device(
    sizes,
    resid_x,
    resid_y,
    face_weights,
    face_counts,
    neumann,
    schur,
    basis,
    coarse_map,
    column_inverse,
    column_basis,
    top_inverse,
):
    gx_n, gy_n, gz_n = sizes
    layer_n = gx_n * gy_n
    owners = ((gz_n - 1) // 2, gz_n // 2) if gz_n % 2 == 0 else (gz_n // 2,)
    halves = len(owners)
    face, loads = resid_x.shape[3:]
    inner = neumann.shape[3]
    coarse = basis.shape[4]
    subs = neumann.shape[0] * neumann.shape[1]
    rx = resid_x[:, :, 0]
    ry = resid_y[:, :, 0]
    weights = face_weights[:, :, 0]
    counts = face_counts[:, :, 0]
    local = subs * coarse
    inv, cbas = column_inverse[0, 0], column_basis[0, 0]
    nc2, nc3 = inv.shape[1], top_inverse.shape[0]
    width = loads // halves
    slab = nc3 // layer_n
    dma = pltpu.SemaphoreType.DMA
    vm = pltpu.VMEM
    nx, ny = rx.shape[1], ry.shape[0]
    spec = pl.BlockSpec(memory_space=pltpu.VMEM)
    hbm = pl.BlockSpec(memory_space=pl.ANY)
    zx, zy = pl.pallas_call(
        functools.partial(kernel, sizes, owners),
        out_shape=(
            jax.ShapeDtypeStruct(rx.shape, F32),
            jax.ShapeDtypeStruct(ry.shape, F32),
        ),
        in_specs=[hbm, hbm, spec, spec, hbm, spec, spec, spec, spec, hbm],
        out_specs=(spec, spec),
        scratch_shapes=[
            vm(rx.shape, F32),
            vm(ry.shape, F32),
            vm((subs, inner, inner), BF16),
            vm(top_inverse.shape, F32),
            vm((subs, inner, 1), F32),
            vm((8, local), jnp.int32),
            vm((2, nx, face, loads), F32),
            vm((2, ny, face, loads), F32),
            vm((2, nx, face, loads), F32),
            vm((2, ny, face, loads), F32),
            vm((subs, inner, loads), BF16),
            vm((subs, inner, loads), F32),
            vm((halves, local, width), F32),
            vm((gz_n, local, width), F32),
            vm((gz_n, 8, local), jnp.int32),
            vm((nc2, nc2), F32),
            vm((nc2, nc3), F32),
            vm((nc3, width), F32),
            vm((gx_n - 1, nc3 // gx_n, width), F32),
            vm((nc3 // gx_n, width), F32),
            vm((gy_n - 1, slab, width), F32),
            vm((slab, width), F32),
            vm((nc3, width), F32),
            vm((gz_n, local, width), F32),
            vm((halves, local, width), F32),
            dma((halves, 4)),
            dma((halves, 4)),
            dma((halves, 4)),
            dma((halves, 4)),
            dma((halves, 3)),
            dma((3, gz_n)),
            dma((halves,)),
            dma((gz_n,)),
            dma((gx_n - 1,)),
            dma((gx_n - 1,)),
            dma((gy_n - 1,)),
            dma((gy_n - 1,)),
            dma((gy_n - 1,)),
            dma((gy_n - 1,)),
            dma((gx_n - 1,)),
            dma((gx_n - 1,)),
            dma((gz_n,)),
            dma((halves,)),
            dma((4,)),
        ],
        compiler_params=pltpu.CompilerParams(
            collective_id=0, has_side_effects=True, vmem_limit_bytes=56 * 1024 * 1024
        ),
        name="bddc",
    )(
        rx,
        ry,
        weights,
        counts,
        neumann.reshape(subs, inner, inner),
        basis.reshape(subs, inner, coarse),
        coarse_map[:, :, 0],
        inv,
        cbas,
        top_inverse,
    )

    def part_of(shape):
        block = shape[:-1] + (width,)
        return pl.BlockSpec(block, lambda k: (0,) * (len(shape) - 1) + (k,))

    def whole(shape):
        return pl.BlockSpec(shape, lambda k: (0,) * len(shape))

    image_shape = (subs, inner, loads)
    z_x, z_y, image = pl.pallas_call(
        image_kernel,
        grid=(halves,),
        out_shape=(
            jax.ShapeDtypeStruct(rx.shape, F32),
            jax.ShapeDtypeStruct(ry.shape, F32),
            jax.ShapeDtypeStruct(image_shape, BF16),
        ),
        in_specs=[
            part_of(rx.shape),
            part_of(ry.shape),
            whole(counts.shape),
            whole((subs, inner, inner)),
        ],
        out_specs=(part_of(rx.shape), part_of(ry.shape), part_of(image_shape)),
        compiler_params=pltpu.CompilerParams(vmem_limit_bytes=48 * 1024 * 1024),
        name="schur_image",
    )(zx, zy, counts, schur.reshape(subs, inner, inner))
    return (
        z_x[:, :, None],
        z_y[:, :, None],
        image.reshape(neumann.shape[0], neumann.shape[1], 1, inner, loads),
    )


def solution(mesh):
    sizes = tuple(mesh.shape[a] for a in AXES)
    vec, mat = P("gx", "gy", "gz", None), P("gx", "gy", "gz", None, None)
    return jax.shard_map(
        functools.partial(on_device, sizes),
        mesh=mesh,
        in_specs=(mat, mat, mat, vec, mat, mat, mat, vec, vec, vec, P()),
        out_specs=(mat, mat, mat),
        check_vma=False,
    )
```

```python
import functools

import jax
import jax.numpy as jnp
from jax import lax
from jax.experimental import pallas as pl
from jax.experimental.pallas import tpu as pltpu
from jax.sharding import PartitionSpec as P

BLK = 30
AXES = ("gx", "gy", "gz")
MESH = pl.DeviceIdType.MESH
F32 = jnp.float32
BF16 = jnp.bfloat16


def mm(a, b):
    return jnp.dot(a.astype(BF16), b.astype(BF16), preferred_element_type=F32)


def live_mask(counts, i, j, face):
    index = lax.broadcasted_iota(jnp.int32, (face, counts.shape[2]), 0)
    return (index < counts[i, j : j + 1] * BLK).astype(F32)


def column(faces):
    return jnp.concatenate([faces[:, k : k + 1] for k in range(faces.shape[1])], 0)


def stack_faces(xf, yf, i, j):
    return jnp.concatenate([xf(i, j), xf(i + 1, j), yf(i, j), yf(i, j + 1)], 0)


def mm_t(a, b):
    return lax.dot_general(
        a.astype(BF16), b.astype(BF16), (((0,), (0,)), ((), ())), preferred_element_type=F32
    )


def kernel(
    sizes,
    owners,
    rx_hbm,
    ry_hbm,
    weights,
    counts,
    neumann_hbm,
    basis,
    targets,
    inv,
    cbas,
    top_hbm,
    zx,
    zy,
    rx,
    ry,
    neumann,
    top,
    scale,
    cmap,
    hx1,
    hy1,
    hx2,
    hy2,
    ubuf,
    wbuf,
    graw,
    raw,
    maps,
    minv,
    mbas,
    g3p,
    rs1,
    sum1,
    rs2,
    part,
    g3,
    vout,
    vall,
    h1_s,
    h1_r,
    h2_s,
    h2_r,
    mat_s,
    mat_r,
    raw_s,
    raw_r,
    rs1_s,
    rs1_r,
    rs2_s,
    rs2_r,
    ag1_s,
    ag1_r,
    ag2_s,
    ag2_r,
    v_s,
    v_r,
    in_s,
):
    gx_n, gy_n, gz_n = sizes
    x, y, z = (lax.axis_index(a) for a in AXES)
    layer_n = gx_n * gy_n
    mine = x * gy_n + y
    halves = len(owners)
    width = rx.shape[3] // halves
    ni, nj = rx.shape[0] - 1, ry.shape[1] - 1
    coarse = basis.shape[1]
    pieces = 2 if width % 256 == 0 else 1
    piece = width // pieces
    rows = inv.shape[0]
    slab = part.shape[0]

    def cols(h):
        return pl.ds(pl.multiple_of(h * width, width), width)

    def copy(src, dst, send, recv, to):
        return pltpu.make_async_remote_copy(
            src_ref=src, dst_ref=dst, send_sem=send, recv_sem=recv, device_id=to, device_id_type=MESH
        )

    def layer_peer(d):
        p = lax.rem(mine + d, layer_n)
        return (p // gy_n, lax.rem(p, gy_n), z)

    loads_in = [
        pltpu.make_async_copy(a, b, in_s.at[k])
        for k, (a, b) in enumerate(
            ((rx_hbm, rx), (ry_hbm, ry), (neumann_hbm, neumann), (top_hbm, top))
        )
    ]
    for c in loads_in:
        c.start()
    lists = [targets[i, j : j + 1] for i in range(ni) for j in range(nj)]
    cmap[...] = jnp.broadcast_to(jnp.concatenate(lists, 1), cmap.shape)

    barrier = pltpu.get_barrier_semaphore()
    for d in range(1, layer_n):
        pl.semaphore_signal(barrier, inc=1, device_id=layer_peer(d), device_id_type=MESH)
    for d in range(1, gz_n):
        pl.semaphore_signal(
            barrier, inc=1, device_id=(x, y, lax.rem(z + d, gz_n)), device_id_type=MESH
        )
    pl.semaphore_wait(barrier, layer_n - 1 + gz_n - 1)

    x_up, x_down = (lax.rem(x + 1, gx_n), y, z), (lax.rem(x + gx_n - 1, gx_n), y, z)
    y_up, y_down = (x, lax.rem(y + 1, gy_n), z), (x, lax.rem(y + gy_n - 1, gy_n), z)

    def halo(fx, fy, hx, hy, send, recv, c, k):
        s, r = send.at[k], recv.at[k]
        return [
            copy(fy.at[:, nj, :, c], hy.at[0, :, :, c], s.at[0], r.at[0], y_up),
            copy(fy.at[:, 0, :, c], hy.at[1, :, :, c], s.at[1], r.at[1], y_down),
            copy(fx.at[ni, :, :, c], hx.at[0, :, :, c], s.at[2], r.at[2], x_up),
            copy(fx.at[0, :, :, c], hx.at[1, :, :, c], s.at[3], r.at[3], x_down),
        ]

    own_rows = pl.ds(pl.multiple_of(z * rows, rows), rows)

    def matrices(k):
        to = (x, y, owners[k])
        return [
            copy(cbas, mbas.at[own_rows], mat_s.at[k, 1], mat_r.at[1, z], to),
            copy(cmap, maps.at[z], mat_s.at[k, 2], mat_r.at[2, z], to),
            copy(inv, minv.at[own_rows], mat_s.at[k, 0], mat_r.at[0, z], to),
        ]

    first = [halo(rx_hbm, ry_hbm, hx1, hy1, h1_s, h1_r, cols(h), h) for h in range(halves)]
    for c in first[0]:
        c.start()
    for k in range(halves):

        @pl.when(z != owners[k])
        def _():
            for c in matrices(k)[:2]:
                c.start()

        @pl.when(z == owners[k])
        def _():
            minv[own_rows] = inv[...]
            mbas[own_rows] = cbas[...]
            maps[z] = cmap[...]

    for i in range(ni):
        for j in range(nj):
            scale[i * nj + j] = column(weights[i, j].T * live_mask(counts, i, j, rx.shape[2]))
    loads_in[0].wait()
    loads_in[1].wait()

    for h in range(halves):
        c = cols(h)
        for f in first[h]:
            f.wait_recv()
        if h + 1 < halves:
            for f in first[h + 1]:
                f.start()

        def xf(q, j):
            own = rx[q, j, :, c]
            return own if 0 < q < ni else own + hx1[0 if q == 0 else 1, j, :, c]

        def yf(i, q):
            own = ry[i, q, :, c]
            return own if 0 < q < nj else own + hy1[0 if q == 0 else 1, i, :, c]

        for i in range(ni):
            for j in range(nj):
                s = i * nj + j
                u = (stack_faces(xf, yf, i, j) * scale[s]).astype(BF16)
                ubuf[s, :, c] = u
                graw[h, s * coarse : (s + 1) * coarse] = mm(basis[s], u)
        o = owners[h]

        @pl.when(z != o)
        def _():
            copy(graw.at[h], raw.at[z], raw_s.at[h], raw_r.at[z], (x, y, o)).start()

        @pl.when(z == o)
        def _():
            raw[z] = graw[h]

        if h == halves - 1:
            for k in range(halves):

                @pl.when(z != owners[k])
                def _():
                    matrices(k)[2].start()

        if h == 0:
            loads_in[2].wait()
        for s in range(ni * nj):
            wbuf[s, :, c] = jnp.dot(neumann[s], ubuf[s, :, c], preferred_element_type=F32)


    def select(zz):
        picks = lax.broadcasted_iota(jnp.int32, (minv.shape[0], cmap.shape[1]), 0)
        return (picks == maps[zz, 0:1]).astype(F32).astype(BF16)

    loads_in[3].wait()
    which = z - owners[0]
    is_owner = (z >= owners[0]) & (z <= owners[-1])

    def far(zz):
        if zz < owners[0]:
            return z > owners[0]
        return z < owners[-1] if zz > owners[-1] else z < 0

    def back(zz, p):
        c = pl.ds(p * piece, piece)
        return copy(
            vout.at[zz, :, c], vall.at[which, :, c], v_s.at[zz, p], v_r.at[which, p], (x, y, zz)
        )

    @pl.when(is_owner)
    def _():
        for zz in range(gz_n):

            @pl.when(z != zz)
            def _():
                copy(graw.at[0], raw.at[zz], raw_s.at[0], raw_r.at[zz], (x, y, zz)).wait_recv()
                there = pl.ds(zz * rows, rows)
                copy(cmap, maps.at[zz], mat_s.at[0, 2], mat_r.at[2, zz], (x, y, zz)).wait_recv()
                copy(cbas, mbas.at[there], mat_s.at[0, 1], mat_r.at[1, zz], (x, y, zz)).wait_recv()

        g2 = lax.fori_loop(
            0,
            gz_n,
            lambda zz, acc: acc + mm(select(zz), raw[zz]),
            jnp.zeros((minv.shape[0], width), F32),
        ).astype(BF16)
        g3p[...] = mm_t(mbas[...], g2)

        def x_peer(d):
            return (lax.rem(x + d, gx_n), y, z)

        def y_peer(d):
            return (x, lax.rem(y + d, gy_n), z)

        half = slab * gy_n
        own_half = pl.ds(pl.multiple_of(x * half, half), half)
        own_part = pl.ds(pl.multiple_of(y * slab, slab), slab)
        own_slab = pl.ds(pl.multiple_of(mine * slab, slab), slab)

        def scatter_x(d):
            to = x_peer(d)
            there = pl.ds(pl.multiple_of(to[0] * half, half), half)
            return copy(g3p.at[there], rs1.at[d - 1], rs1_s.at[d - 1], rs1_r.at[d - 1], to)

        def scatter_y(d):
            to = y_peer(d)
            there = pl.ds(pl.multiple_of(to[1] * slab, slab), slab)
            return copy(sum1.at[there], rs2.at[d - 1], rs2_s.at[d - 1], rs2_r.at[d - 1], to)

        def gather_y(d, source):
            rows_y = pl.ds(pl.multiple_of((x * gy_n + source) * slab, slab), slab)
            return copy(part, g3.at[rows_y], ag1_s.at[d - 1], ag1_r.at[d - 1], y_peer(d))

        def gather_x(d, source):
            rows_x = pl.ds(pl.multiple_of(source * half, half), half)
            return copy(g3.at[own_half], g3.at[rows_x], ag2_s.at[d - 1], ag2_r.at[d - 1], x_peer(d))

        for d in range(1, gx_n):
            scatter_x(d).start()
        total = g3p[own_half]
        for d in range(1, gx_n):
            scatter_x(d).wait_recv()
            total = total + rs1[d - 1]
        sum1[...] = total
        for d in range(1, gy_n):
            scatter_y(d).start()
        total = sum1[own_part]
        for d in range(1, gy_n):
            scatter_y(d).wait_recv()
            total = total + rs2[d - 1]
        part[...] = total
        g3[own_slab] = total
        for d in range(1, gy_n):
            gather_y(d, y).start()
        for d in range(1, gy_n):
            gather_y(d, lax.rem(y + gy_n - d, gy_n)).wait_recv()
        for d in range(1, gx_n):
            gather_x(d, x).start()
        for zz in range(gz_n):

            @pl.when(z != zz)
            def _():
                there = pl.ds(zz * rows, rows)
                copy(inv, minv.at[there], mat_s.at[0, 0], mat_r.at[0, zz], (x, y, zz)).wait_recv()

        y2 = mm(minv[...], g2)
        for d in range(1, gx_n):
            gather_x(d, lax.rem(x + gx_n - d, gx_n)).wait_recv()
        y3 = mm(top[...], g3[...])
        v2 = (y2 + mm(mbas[...], y3)).astype(BF16)
        for zz in range(gz_n):
            vout[zz] = mm_t(select(zz), v2)

            @pl.when((z != zz) & jnp.logical_not(far(zz)))
            def _():
                back(zz, 0).start()

            @pl.when(z == zz)
            def _():
                vall[which] = vout[zz]

        for zz in range(gz_n):

            @pl.when((z != zz) & jnp.logical_not(far(zz)))
            def _():
                for p in range(1, pieces):
                    back(zz, p).start()

        for d in range(1, gx_n):
            scatter_x(d).wait_send()
            gather_x(d, x).wait_send()
        for d in range(1, gy_n):
            scatter_y(d).wait_send()
            gather_y(d, y).wait_send()

    turn = z // ((gz_n + 1) // 2) if halves > 1 else 0
    order = [lax.rem(k + turn, halves) for k in range(halves)]
    spots = [(k, h, p) for k, h in enumerate(order) for p in range(pieces)]
    spans = [
        pl.ds(pl.multiple_of(h * width + p * piece, piece), piece) for k, h, p in spots
    ]
    second = [
        halo(zx, zy, hx2, hy2, h2_s, h2_r, c, h * pieces + p)
        for (k, h, p), c in zip(spots, spans)
    ]
    face = rx.shape[2]
    for n, (k, h, p) in enumerate(spots):
        c = spans[n]
        within = pl.ds(p * piece, piece)
        o = owners[0] + h

        @pl.when(z != o)
        def _():
            copy(
                vout.at[0, :, within], vall.at[h, :, within], v_s.at[0, p], v_r.at[h, p], (x, y, o)
            ).wait_recv()

        for i in range(ni):
            for j in range(nj):
                s = i * nj + j
                v = vall[h, s * coarse : (s + 1) * coarse, within].astype(BF16)
                con = (wbuf[s, :, c] + mm_t(basis[s], v)) * scale[s]
                c0, c1, c2, c3 = (con[m * face : (m + 1) * face] for m in range(4))
                zx[i, j, :, c] = c0 if i == 0 else zx[i, j, :, c] + c0
                zx[i + 1, j, :, c] = c1
                zy[i, j, :, c] = c2 if j == 0 else zy[i, j, :, c] + c2
                zy[i, j + 1, :, c] = c3
        for f in second[n]:
            f.start()
        if k == 0 and p == pieces - 1:

            @pl.when(is_owner)
            def _():
                for zz in range(gz_n):

                    @pl.when((z != zz) & jnp.logical_not(far(zz)))
                    def _():
                        for q in range(pieces):
                            back(zz, q).wait_send()

                for zz in range(gz_n):

                    @pl.when(far(zz))
                    def _():
                        for q in range(pieces):
                            back(zz, q).start()

    for n, c in enumerate(spans):
        for f in second[n]:
            f.wait()
        for j in range(nj):
            zx[0, j, :, c] += hx2[0, j, :, c]
            zx[ni, j, :, c] += hx2[1, j, :, c]
        for i in range(ni):
            zy[i, 0, :, c] += hy2[0, i, :, c]
            zy[i, nj, :, c] += hy2[1, i, :, c]

    for h in range(halves):
        for f in first[h]:
            f.wait_send()
        o = owners[h]

        @pl.when(z != o)
        def _():
            for f in matrices(h):
                f.wait_send()
            copy(graw.at[h], raw.at[z], raw_s.at[h], raw_r.at[z], (x, y, o)).wait_send()

    @pl.when(is_owner)
    def _():
        for zz in range(gz_n):

            @pl.when(far(zz))
            def _():
                for q in range(pieces):
                    back(zz, q).wait_send()


def image_kernel(zx, zy, counts, schur, out_x, out_y, image):
    out_x[...] = zx[...]
    out_y[...] = zy[...]
    ni, nj = zx.shape[0] - 1, zy.shape[1] - 1
    for i in range(ni):
        for j in range(nj):
            s = i * nj + j
            zs = stack_faces(lambda q, jj: zx[q, jj], lambda ii, q: zy[ii, q], i, j)
            zs = (zs * column(live_mask(counts, i, j, zx.shape[2]))).astype(BF16)
            image[s] = jnp.dot(schur[s], zs, preferred_element_type=F32).astype(BF16)


def on_device(
    sizes,
    resid_x,
    resid_y,
    face_weights,
    face_counts,
    neumann,
    schur,
    basis,
    coarse_map,
    column_inverse,
    column_basis,
    top_inverse,
):
    gx_n, gy_n, gz_n = sizes
    layer_n = gx_n * gy_n
    owners = ((gz_n - 1) // 2, gz_n // 2) if gz_n % 2 == 0 else (gz_n // 2,)
    halves = len(owners)
    face, loads = resid_x.shape[3:]
    inner = neumann.shape[3]
    coarse = basis.shape[4]
    subs = neumann.shape[0] * neumann.shape[1]
    rx = resid_x[:, :, 0]
    ry = resid_y[:, :, 0]
    weights = face_weights[:, :, 0]
    counts = face_counts[:, :, 0]
    local = subs * coarse
    inv, cbas = column_inverse[0, 0], column_basis[0, 0]
    nc2, nc3 = inv.shape[1], top_inverse.shape[0]
    width = loads // halves
    pieces = 2 if width % 256 == 0 else 1
    slab = nc3 // layer_n
    dma = pltpu.SemaphoreType.DMA
    vm = pltpu.VMEM
    nx, ny = rx.shape[1], ry.shape[0]
    spec = pl.BlockSpec(memory_space=pltpu.VMEM)
    hbm = pl.BlockSpec(memory_space=pl.ANY)
    zx, zy = pl.pallas_call(
        functools.partial(kernel, sizes, owners),
        out_shape=(
            jax.ShapeDtypeStruct(rx.shape, F32),
            jax.ShapeDtypeStruct(ry.shape, F32),
        ),
        in_specs=[hbm, hbm, spec, spec, hbm, spec, spec, spec, spec, hbm],
        out_specs=(spec, spec),
        scratch_shapes=[
            vm(rx.shape, F32),
            vm(ry.shape, F32),
            vm((subs, inner, inner), BF16),
            vm(top_inverse.shape, F32),
            vm((subs, inner, 1), F32),
            vm((8, local), jnp.int32),
            vm((2, nx, face, loads), F32),
            vm((2, ny, face, loads), F32),
            vm((2, nx, face, loads), F32),
            vm((2, ny, face, loads), F32),
            vm((subs, inner, loads), BF16),
            vm((subs, inner, loads), F32),
            vm((halves, local, width), F32),
            vm((gz_n, local, width), F32),
            vm((gz_n, 8, local), jnp.int32),
            vm((nc2, nc2), F32),
            vm((nc2, nc3), F32),
            vm((nc3, width), F32),
            vm((gx_n - 1, nc3 // gx_n, width), F32),
            vm((nc3 // gx_n, width), F32),
            vm((gy_n - 1, slab, width), F32),
            vm((slab, width), F32),
            vm((nc3, width), F32),
            vm((gz_n, local, width), F32),
            vm((halves, local, width), F32),
            dma((halves, 4)),
            dma((halves, 4)),
            dma((halves * pieces, 4)),
            dma((halves * pieces, 4)),
            dma((halves, 3)),
            dma((3, gz_n)),
            dma((halves,)),
            dma((gz_n,)),
            dma((gx_n - 1,)),
            dma((gx_n - 1,)),
            dma((gy_n - 1,)),
            dma((gy_n - 1,)),
            dma((gy_n - 1,)),
            dma((gy_n - 1,)),
            dma((gx_n - 1,)),
            dma((gx_n - 1,)),
            dma((gz_n, pieces)),
            dma((halves, pieces)),
            dma((4,)),
        ],
        compiler_params=pltpu.CompilerParams(
            collective_id=0, has_side_effects=True, vmem_limit_bytes=56 * 1024 * 1024
        ),
        name="bddc",
    )(
        rx,
        ry,
        weights,
        counts,
        neumann.reshape(subs, inner, inner),
        jnp.swapaxes(basis, 3, 4).reshape(subs, coarse, inner),
        coarse_map[:, :, 0],
        inv,
        cbas,
        top_inverse,
    )

    def part_of(shape):
        block = shape[:-1] + (width,)
        return pl.BlockSpec(block, lambda k: (0,) * (len(shape) - 1) + (k,))

    def whole(shape):
        return pl.BlockSpec(shape, lambda k: (0,) * len(shape))

    image_shape = (subs, inner, loads)
    z_x, z_y, image = pl.pallas_call(
        image_kernel,
        grid=(halves,),
        out_shape=(
            jax.ShapeDtypeStruct(rx.shape, F32),
            jax.ShapeDtypeStruct(ry.shape, F32),
            jax.ShapeDtypeStruct(image_shape, BF16),
        ),
        in_specs=[
            part_of(rx.shape),
            part_of(ry.shape),
            whole(counts.shape),
            whole((subs, inner, inner)),
        ],
        out_specs=(part_of(rx.shape), part_of(ry.shape), part_of(image_shape)),
        compiler_params=pltpu.CompilerParams(vmem_limit_bytes=60 * 1024 * 1024),
        name="schur_image",
    )(zx, zy, counts, schur.reshape(subs, inner, inner))
    return (
        z_x[:, :, None],
        z_y[:, :, None],
        image.reshape(neumann.shape[0], neumann.shape[1], 1, inner, loads),
    )


def solution(mesh):
    sizes = tuple(mesh.shape[a] for a in AXES)
    vec, mat = P("gx", "gy", "gz", None), P("gx", "gy", "gz", None, None)
    return jax.shard_map(
        functools.partial(on_device, sizes),
        mesh=mesh,
        in_specs=(mat, mat, mat, vec, mat, mat, mat, vec, vec, vec, P()),
        out_specs=(mat, mat, mat),
        check_vma=False,
    )
```

```python
import functools

import jax
import jax.numpy as jnp
from jax import lax
from jax.experimental import pallas as pl
from jax.experimental.pallas import tpu as pltpu
from jax.sharding import PartitionSpec as P

BLK = 30
AXES = ("gx", "gy", "gz")
MESH = pl.DeviceIdType.MESH
F32 = jnp.float32
BF16 = jnp.bfloat16


def mm(a, b):
    return jnp.dot(a.astype(BF16), b.astype(BF16), preferred_element_type=F32)


def live_mask(counts, i, j, face):
    index = lax.broadcasted_iota(jnp.int32, (face, counts.shape[2]), 0)
    return (index < counts[i, j : j + 1] * BLK).astype(F32)


def column(faces):
    return jnp.concatenate([faces[:, k : k + 1] for k in range(faces.shape[1])], 0)


def stack_faces(xf, yf, i, j):
    return jnp.concatenate([xf(i, j), xf(i + 1, j), yf(i, j), yf(i, j + 1)], 0)


def mm_t(a, b):
    return lax.dot_general(
        a.astype(BF16), b.astype(BF16), (((0,), (0,)), ((), ())), preferred_element_type=F32
    )


def kernel(
    sizes,
    owners,
    rx_hbm,
    ry_hbm,
    weights,
    counts,
    neumann_hbm,
    basis,
    targets,
    inv,
    cbas,
    top_hbm,
    zx,
    zy,
    rx,
    ry,
    neumann,
    top,
    scale,
    cmap,
    hx1,
    hy1,
    hx2,
    hy2,
    ubuf,
    wbuf,
    graw,
    raw,
    maps,
    minv,
    mbas,
    g3p,
    rs1,
    sum1,
    rs2,
    part,
    g3,
    vout,
    vall,
    h1_s,
    h1_r,
    h2_s,
    h2_r,
    mat_s,
    mat_r,
    raw_s,
    raw_r,
    rs1_s,
    rs1_r,
    rs2_s,
    rs2_r,
    ag1_s,
    ag1_r,
    ag2_s,
    ag2_r,
    v_s,
    v_r,
    in_s,
):
    gx_n, gy_n, gz_n = sizes
    x, y, z = (lax.axis_index(a) for a in AXES)
    layer_n = gx_n * gy_n
    mine = x * gy_n + y
    halves = len(owners)
    width = rx.shape[3] // halves
    ni, nj = rx.shape[0] - 1, ry.shape[1] - 1
    coarse = basis.shape[1]
    pieces = 2 if width % 256 == 0 else 1
    piece = width // pieces
    rows = inv.shape[0]
    slab = part.shape[0]

    def cols(h):
        return pl.ds(pl.multiple_of(h * width, width), width)

    def copy(src, dst, send, recv, to):
        return pltpu.make_async_remote_copy(
            src_ref=src, dst_ref=dst, send_sem=send, recv_sem=recv, device_id=to, device_id_type=MESH
        )

    def layer_peer(d):
        p = lax.rem(mine + d, layer_n)
        return (p // gy_n, lax.rem(p, gy_n), z)

    loads_in = [
        pltpu.make_async_copy(a, b, in_s.at[k])
        for k, (a, b) in enumerate(
            ((rx_hbm, rx), (ry_hbm, ry), (neumann_hbm, neumann), (top_hbm, top))
        )
    ]
    for c in loads_in:
        c.start()
    lists = [targets[i, j : j + 1] for i in range(ni) for j in range(nj)]
    cmap[...] = jnp.broadcast_to(jnp.concatenate(lists, 1), cmap.shape)

    barrier = pltpu.get_barrier_semaphore()
    for d in range(1, layer_n):
        pl.semaphore_signal(barrier, inc=1, device_id=layer_peer(d), device_id_type=MESH)
    for d in range(1, gz_n):
        pl.semaphore_signal(
            barrier, inc=1, device_id=(x, y, lax.rem(z + d, gz_n)), device_id_type=MESH
        )
    pl.semaphore_wait(barrier, layer_n - 1 + gz_n - 1)

    x_up, x_down = (lax.rem(x + 1, gx_n), y, z), (lax.rem(x + gx_n - 1, gx_n), y, z)
    y_up, y_down = (x, lax.rem(y + 1, gy_n), z), (x, lax.rem(y + gy_n - 1, gy_n), z)

    def halo(fx, fy, hx, hy, send, recv, c, k):
        s, r = send.at[k], recv.at[k]
        return [
            copy(fy.at[:, nj, :, c], hy.at[0, :, :, c], s.at[0], r.at[0], y_up),
            copy(fy.at[:, 0, :, c], hy.at[1, :, :, c], s.at[1], r.at[1], y_down),
            copy(fx.at[ni, :, :, c], hx.at[0, :, :, c], s.at[2], r.at[2], x_up),
            copy(fx.at[0, :, :, c], hx.at[1, :, :, c], s.at[3], r.at[3], x_down),
        ]

    own_rows = pl.ds(pl.multiple_of(z * rows, rows), rows)

    def matrices(k):
        to = (x, y, owners[k])
        return [
            copy(cbas, mbas.at[own_rows], mat_s.at[k, 1], mat_r.at[1, z], to),
            copy(cmap, maps.at[z], mat_s.at[k, 2], mat_r.at[2, z], to),
            copy(inv, minv.at[own_rows], mat_s.at[k, 0], mat_r.at[0, z], to),
        ]

    first = [halo(rx_hbm, ry_hbm, hx1, hy1, h1_s, h1_r, cols(h), h) for h in range(halves)]
    for c in first[0]:
        c.start()
    for k in range(halves):

        @pl.when(z != owners[k])
        def _():
            for c in matrices(k)[:2]:
                c.start()

        @pl.when(z == owners[k])
        def _():
            minv[own_rows] = inv[...]
            mbas[own_rows] = cbas[...]
            maps[z] = cmap[...]

    for i in range(ni):
        for j in range(nj):
            scale[i * nj + j] = column(weights[i, j].T * live_mask(counts, i, j, rx.shape[2]))
    loads_in[0].wait()
    loads_in[1].wait()

    for h in range(halves):
        c = cols(h)
        if h + 1 < halves:
            for f, g in zip(first[h], first[h + 1]):
                f.wait_send()
                g.start()
        for f in first[h]:
            f.wait_recv()

        def xf(q, j):
            own = rx[q, j, :, c]
            return own if 0 < q < ni else own + hx1[0 if q == 0 else 1, j, :, c]

        def yf(i, q):
            own = ry[i, q, :, c]
            return own if 0 < q < nj else own + hy1[0 if q == 0 else 1, i, :, c]

        for i in range(ni):
            for j in range(nj):
                s = i * nj + j
                u = (stack_faces(xf, yf, i, j) * scale[s]).astype(BF16)
                ubuf[s, :, c] = u
                graw[h, s * coarse : (s + 1) * coarse] = mm(basis[s], u)
        o = owners[h]

        @pl.when(z != o)
        def _():
            copy(graw.at[h], raw.at[z], raw_s.at[h], raw_r.at[z], (x, y, o)).start()

        @pl.when(z == o)
        def _():
            raw[z] = graw[h]

        if h == 0:
            loads_in[2].wait()
        for s in range(ni * nj):
            wbuf[s, :, c] = jnp.dot(neumann[s], ubuf[s, :, c], preferred_element_type=F32)

    def to_owner(h):
        return copy(graw.at[h], raw.at[z], raw_s.at[h], raw_r.at[z], (x, y, owners[h]))

    @pl.when(z != owners[-1])
    def _():
        to_owner(halves - 1).wait_send()

    for k in range(halves):

        @pl.when(z != owners[k])
        def _():
            matrices(k)[2].start()


    def select(zz):
        picks = lax.broadcasted_iota(jnp.int32, (minv.shape[0], cmap.shape[1]), 0)
        return (picks == maps[zz, 0:1]).astype(F32).astype(BF16)

    loads_in[3].wait()
    which = z - owners[0]
    is_owner = (z >= owners[0]) & (z <= owners[-1])

    def far(zz):
        if zz < owners[0]:
            return z > owners[0]
        return z < owners[-1] if zz > owners[-1] else z < 0

    def back(zz, p):
        c = pl.ds(p * piece, piece)
        return copy(
            vout.at[zz, :, c], vall.at[which, :, c], v_s.at[zz, p], v_r.at[which, p], (x, y, zz)
        )

    @pl.when(is_owner)
    def _():
        for zz in range(gz_n):

            @pl.when(z != zz)
            def _():
                copy(graw.at[0], raw.at[zz], raw_s.at[0], raw_r.at[zz], (x, y, zz)).wait_recv()
                there = pl.ds(zz * rows, rows)
                copy(cmap, maps.at[zz], mat_s.at[0, 2], mat_r.at[2, zz], (x, y, zz)).wait_recv()
                copy(cbas, mbas.at[there], mat_s.at[0, 1], mat_r.at[1, zz], (x, y, zz)).wait_recv()

        g2 = lax.fori_loop(
            0,
            gz_n,
            lambda zz, acc: acc + mm(select(zz), raw[zz]),
            jnp.zeros((minv.shape[0], width), F32),
        ).astype(BF16)
        g3p[...] = mm_t(mbas[...], g2)

        def x_peer(d):
            return (lax.rem(x + d, gx_n), y, z)

        def y_peer(d):
            return (x, lax.rem(y + d, gy_n), z)

        half = slab * gy_n
        own_half = pl.ds(pl.multiple_of(x * half, half), half)
        own_part = pl.ds(pl.multiple_of(y * slab, slab), slab)
        own_slab = pl.ds(pl.multiple_of(mine * slab, slab), slab)

        def scatter_x(d):
            to = x_peer(d)
            there = pl.ds(pl.multiple_of(to[0] * half, half), half)
            return copy(g3p.at[there], rs1.at[d - 1], rs1_s.at[d - 1], rs1_r.at[d - 1], to)

        def scatter_y(d):
            to = y_peer(d)
            there = pl.ds(pl.multiple_of(to[1] * slab, slab), slab)
            return copy(sum1.at[there], rs2.at[d - 1], rs2_s.at[d - 1], rs2_r.at[d - 1], to)

        def gather_y(d, source):
            rows_y = pl.ds(pl.multiple_of((x * gy_n + source) * slab, slab), slab)
            return copy(part, g3.at[rows_y], ag1_s.at[d - 1], ag1_r.at[d - 1], y_peer(d))

        def gather_x(d, source):
            rows_x = pl.ds(pl.multiple_of(source * half, half), half)
            return copy(g3.at[own_half], g3.at[rows_x], ag2_s.at[d - 1], ag2_r.at[d - 1], x_peer(d))

        for d in range(1, gx_n):
            scatter_x(d).start()
        total = g3p[own_half]
        for d in range(1, gx_n):
            scatter_x(d).wait_recv()
            total = total + rs1[d - 1]
        sum1[...] = total
        for d in range(1, gy_n):
            scatter_y(d).start()
        total = sum1[own_part]
        for d in range(1, gy_n):
            scatter_y(d).wait_recv()
            total = total + rs2[d - 1]
        part[...] = total
        g3[own_slab] = total
        for d in range(1, gy_n):
            gather_y(d, y).start()
        for d in range(1, gy_n):
            gather_y(d, lax.rem(y + gy_n - d, gy_n)).wait_recv()
        for d in range(1, gx_n):
            gather_x(d, x).start()
        for zz in range(gz_n):

            @pl.when(z != zz)
            def _():
                there = pl.ds(zz * rows, rows)
                copy(inv, minv.at[there], mat_s.at[0, 0], mat_r.at[0, zz], (x, y, zz)).wait_recv()

        y2 = mm(minv[...], g2)
        for d in range(1, gx_n):
            gather_x(d, lax.rem(x + gx_n - d, gx_n)).wait_recv()
        y3 = mm(top[...], g3[...])
        v2 = (y2 + mm(mbas[...], y3)).astype(BF16)
        for zz in range(gz_n):
            vout[zz] = mm_t(select(zz), v2)

            @pl.when((z != zz) & jnp.logical_not(far(zz)))
            def _():
                back(zz, 0).start()

            @pl.when(z == zz)
            def _():
                vall[which] = vout[zz]

        for zz in range(gz_n):

            @pl.when((z != zz) & jnp.logical_not(far(zz)))
            def _():
                for p in range(1, pieces):
                    back(zz, p).start()

        for d in range(1, gx_n):
            scatter_x(d).wait_send()
            gather_x(d, x).wait_send()
        for d in range(1, gy_n):
            scatter_y(d).wait_send()
            gather_y(d, y).wait_send()

    turn = z // ((gz_n + 1) // 2) if halves > 1 else 0
    order = [lax.rem(k + turn, halves) for k in range(halves)]
    spots = [(k, h, p) for k, h in enumerate(order) for p in range(pieces)]
    spans = [
        pl.ds(pl.multiple_of(h * width + p * piece, piece), piece) for k, h, p in spots
    ]
    second = [
        halo(zx, zy, hx2, hy2, h2_s, h2_r, c, h * pieces + p)
        for (k, h, p), c in zip(spots, spans)
    ]
    face = rx.shape[2]
    for n, (k, h, p) in enumerate(spots):
        c = spans[n]
        within = pl.ds(p * piece, piece)
        o = owners[0] + h

        @pl.when(z != o)
        def _():
            copy(
                vout.at[0, :, within], vall.at[h, :, within], v_s.at[0, p], v_r.at[h, p], (x, y, o)
            ).wait_recv()

        for i in range(ni):
            for j in range(nj):
                s = i * nj + j
                v = vall[h, s * coarse : (s + 1) * coarse, within].astype(BF16)
                con = (wbuf[s, :, c] + mm_t(basis[s], v)) * scale[s]
                c0, c1, c2, c3 = (con[m * face : (m + 1) * face] for m in range(4))
                zx[i, j, :, c] = c0 if i == 0 else zx[i, j, :, c] + c0
                zx[i + 1, j, :, c] = c1
                zy[i, j, :, c] = c2 if j == 0 else zy[i, j, :, c] + c2
                zy[i, j + 1, :, c] = c3
        for f in second[n]:
            f.start()
        if k == 0 and p == pieces - 1:

            @pl.when(is_owner)
            def _():
                for zz in range(gz_n):

                    @pl.when((z != zz) & jnp.logical_not(far(zz)))
                    def _():
                        for q in range(pieces):
                            back(zz, q).wait_send()

                for zz in range(gz_n):

                    @pl.when(far(zz))
                    def _():
                        for q in range(pieces):
                            back(zz, q).start()

    for n, c in enumerate(spans):
        for f in second[n]:
            f.wait()
        for j in range(nj):
            zx[0, j, :, c] += hx2[0, j, :, c]
            zx[ni, j, :, c] += hx2[1, j, :, c]
        for i in range(ni):
            zy[i, 0, :, c] += hy2[0, i, :, c]
            zy[i, nj, :, c] += hy2[1, i, :, c]

    for h in range(halves):
        if h == halves - 1:
            for f in first[h]:
                f.wait_send()
        o = owners[h]

        @pl.when(z != o)
        def _():
            for f in matrices(h):
                f.wait_send()
            if h < halves - 1:
                to_owner(h).wait_send()

    @pl.when(is_owner)
    def _():
        for zz in range(gz_n):

            @pl.when(far(zz))
            def _():
                for q in range(pieces):
                    back(zz, q).wait_send()


def image_kernel(zx, zy, counts, schur, out_x, out_y, image):
    out_x[...] = zx[...]
    out_y[...] = zy[...]
    ni, nj = zx.shape[0] - 1, zy.shape[1] - 1
    for i in range(ni):
        for j in range(nj):
            s = i * nj + j
            zs = stack_faces(lambda q, jj: zx[q, jj], lambda ii, q: zy[ii, q], i, j)
            zs = (zs * column(live_mask(counts, i, j, zx.shape[2]))).astype(BF16)
            image[s] = jnp.dot(schur[s], zs, preferred_element_type=F32).astype(BF16)


def on_device(
    sizes,
    resid_x,
    resid_y,
    face_weights,
    face_counts,
    neumann,
    schur,
    basis,
    coarse_map,
    column_inverse,
    column_basis,
    top_inverse,
):
    gx_n, gy_n, gz_n = sizes
    layer_n = gx_n * gy_n
    owners = ((gz_n - 1) // 2, gz_n // 2) if gz_n % 2 == 0 else (gz_n // 2,)
    halves = len(owners)
    face, loads = resid_x.shape[3:]
    inner = neumann.shape[3]
    coarse = basis.shape[4]
    subs = neumann.shape[0] * neumann.shape[1]
    rx = resid_x[:, :, 0]
    ry = resid_y[:, :, 0]
    weights = face_weights[:, :, 0]
    counts = face_counts[:, :, 0]
    local = subs * coarse
    inv, cbas = column_inverse[0, 0], column_basis[0, 0]
    nc2, nc3 = inv.shape[1], top_inverse.shape[0]
    width = loads // halves
    pieces = 2 if width % 256 == 0 else 1
    slab = nc3 // layer_n
    dma = pltpu.SemaphoreType.DMA
    vm = pltpu.VMEM
    nx, ny = rx.shape[1], ry.shape[0]
    spec = pl.BlockSpec(memory_space=pltpu.VMEM)
    hbm = pl.BlockSpec(memory_space=pl.ANY)
    zx, zy = pl.pallas_call(
        functools.partial(kernel, sizes, owners),
        out_shape=(
            jax.ShapeDtypeStruct(rx.shape, F32),
            jax.ShapeDtypeStruct(ry.shape, F32),
        ),
        in_specs=[hbm, hbm, spec, spec, hbm, spec, spec, spec, spec, hbm],
        out_specs=(spec, spec),
        scratch_shapes=[
            vm(rx.shape, F32),
            vm(ry.shape, F32),
            vm((subs, inner, inner), BF16),
            vm(top_inverse.shape, F32),
            vm((subs, inner, 1), F32),
            vm((8, local), jnp.int32),
            vm((2, nx, face, loads), F32),
            vm((2, ny, face, loads), F32),
            vm((2, nx, face, loads), F32),
            vm((2, ny, face, loads), F32),
            vm((subs, inner, loads), BF16),
            vm((subs, inner, loads), F32),
            vm((halves, local, width), F32),
            vm((gz_n, local, width), F32),
            vm((gz_n, 8, local), jnp.int32),
            vm((nc2, nc2), F32),
            vm((nc2, nc3), F32),
            vm((nc3, width), F32),
            vm((gx_n - 1, nc3 // gx_n, width), F32),
            vm((nc3 // gx_n, width), F32),
            vm((gy_n - 1, slab, width), F32),
            vm((slab, width), F32),
            vm((nc3, width), F32),
            vm((gz_n, local, width), F32),
            vm((halves, local, width), F32),
            dma((halves, 4)),
            dma((halves, 4)),
            dma((halves * pieces, 4)),
            dma((halves * pieces, 4)),
            dma((halves, 3)),
            dma((3, gz_n)),
            dma((halves,)),
            dma((gz_n,)),
            dma((gx_n - 1,)),
            dma((gx_n - 1,)),
            dma((gy_n - 1,)),
            dma((gy_n - 1,)),
            dma((gy_n - 1,)),
            dma((gy_n - 1,)),
            dma((gx_n - 1,)),
            dma((gx_n - 1,)),
            dma((gz_n, pieces)),
            dma((halves, pieces)),
            dma((4,)),
        ],
        compiler_params=pltpu.CompilerParams(
            collective_id=0, has_side_effects=True, vmem_limit_bytes=56 * 1024 * 1024
        ),
        name="bddc",
    )(
        rx,
        ry,
        weights,
        counts,
        neumann.reshape(subs, inner, inner),
        jnp.swapaxes(basis, 3, 4).reshape(subs, coarse, inner),
        coarse_map[:, :, 0],
        inv,
        cbas,
        top_inverse,
    )

    def part_of(shape):
        block = shape[:-1] + (width,)
        return pl.BlockSpec(block, lambda k: (0,) * (len(shape) - 1) + (k,))

    def whole(shape):
        return pl.BlockSpec(shape, lambda k: (0,) * len(shape))

    image_shape = (subs, inner, loads)
    z_x, z_y, image = pl.pallas_call(
        image_kernel,
        grid=(halves,),
        out_shape=(
            jax.ShapeDtypeStruct(rx.shape, F32),
            jax.ShapeDtypeStruct(ry.shape, F32),
            jax.ShapeDtypeStruct(image_shape, BF16),
        ),
        in_specs=[
            part_of(rx.shape),
            part_of(ry.shape),
            whole(counts.shape),
            whole((subs, inner, inner)),
        ],
        out_specs=(part_of(rx.shape), part_of(ry.shape), part_of(image_shape)),
        compiler_params=pltpu.CompilerParams(vmem_limit_bytes=60 * 1024 * 1024),
        name="schur_image",
    )(zx, zy, counts, schur.reshape(subs, inner, inner))
    return (
        z_x[:, :, None],
        z_y[:, :, None],
        image.reshape(neumann.shape[0], neumann.shape[1], 1, inner, loads),
    )


def solution(mesh):
    sizes = tuple(mesh.shape[a] for a in AXES)
    vec, mat = P("gx", "gy", "gz", None), P("gx", "gy", "gz", None, None)
    return jax.shard_map(
        functools.partial(on_device, sizes),
        mesh=mesh,
        in_specs=(mat, mat, mat, vec, mat, mat, mat, vec, vec, vec, P()),
        out_specs=(mat, mat, mat),
        check_vma=False,
    )
```
